32 devices in a mesh: pole: 4 (over x, core), grid: 8 (over z, y).
Axes of the slice: x: 2, y: 2, z: 4, core: 2. Of those that a mesh axis runs over, the one named last changes fastest.
Arguments:
- trailing: bfloat16 [4, 2, 4096, 4096], P('pole', None, 'grid'), may hold values from -4.5 to 4.5, as said below
- panel: bfloat16 [4, 2, 4096, 256], P('pole', None, 'grid'), may hold values from -0.0625 to 0.0625
- diag_inverse: bfloat16 [4, 2, 256, 256], P('pole', None, 'grid'), may hold values from -6 to 6
- pole_weights: float32 [4, 2], P('pole'), may hold values from -3 to 3
- owner_map: int32 [4096, 1], P('grid'), may hold values from 0 to 3; in each aligned block of 512 rows (0 to 511, 512 to 1023, ...) at most 256 rows name the same one
- ham_slab: bfloat16 [256, 4096], replicated, may hold values from -0.375 to 0.375
Outputs:
- density_diag: float32 [256, 256], P('grid')
- patch_energy: bfloat16 [8192, 4096], P(('pole', 'grid'))
The draws below stay inside these ranges and needn't reach their ends.
Inputs may be any that keep to these rules, and one draw needn't show every extreme that they name: trailing is symmetric in its last two dimensions: trailing[p, c, i, j] = trailing[p, c, j, i]. `owner_map`: in each aligned block of 512 rows (the rows of one index of grid) at most 256 rows name the same owner, and some block reaches 256.
All inputs are finite; a program needn't handle non-finite values.
Results may differ from the reference program's by a relative error of at most 0.011.
Values may be sent and summed in bfloat16 or wider, within the bound.
A program may use at most 64 MiB of HBM per device.

```python
import math
import jax
import jax.numpy as jnp
import numpy as np
from jax import lax

M = 4096
W = 256
POLES = 4
RD = 512
CAP = 256
SLOTS = 8192
N_POLE = 4
N_GRID = 8


def draw_trailing(key, part):
    base = jax.random.normal(key, (POLES, 2, M, M), jnp.float32)
    sym = (base + jnp.swapaxes(base, 2, 3)) * math.sqrt(0.5)
    return jnp.clip(sym, -4.5, 4.5).astype(jnp.bfloat16)


def shard_levels(stream_key, extent, cuts, smallest, top_value):
    def one(dim, shards_of):
        heights = jax.random.uniform(jax.random.fold_in(jax.random.fold_in(stream_key, 6), dim), (shards_of,), jnp.float32, smallest / len(cuts), top_value / len(cuts))
        return jnp.repeat(jnp.exp(heights), extent[dim] // shards_of).reshape((-1,) + (1,) * (len(extent) - dim - 1))

    level = one(*cuts[0])
    for cut in cuts[1:]:
        level = level * one(*cut)
    return level


def assign_block(stream_key, own, number, rows, count, top, limit, slope):
    sequence = jax.random.permutation(stream_key, count)
    packed, ordinary = portions_of(count, rows * top, limit, slope, True), portions_of(count, rows * top, limit, slope, False)
    places = jnp.arange(count)

    def named(tallies, offset_by):
        used = int((tallies > 0).sum())
        fixed = max(1, used // 4)
        passed = fixed + (places - fixed + offset_by * (used - fixed)) % max(1, count - fixed)
        return jnp.zeros((count,), jnp.int32).at[sequence[jnp.where(places < fixed, places, passed)]].set(jnp.asarray(tallies, jnp.int32))

    tallies = jnp.where(number % 4 == 0, named(packed, number // 4), named(ordinary, number - number // 4 - 1))
    mixed = jax.random.permutation(jax.random.fold_in(own, 3), count)
    giver, taker = mixed[0:count // 2 * 2:2], mixed[1:count // 2 * 2:2]
    room = jnp.minimum(tallies[giver] - 1, limit - tallies[taker]) // 2
    room = jnp.where((giver == sequence[0]) | (taker == sequence[0]) | (tallies[taker] == 0), 0, jnp.maximum(room, 0))
    passed = jax.random.randint(jax.random.fold_in(own, 4), (count // 2,), 0, 1 << 20) % (room + 1)
    tallies = tallies.at[giver].add(-passed).at[taker].add(passed)
    members = jnp.searchsorted(jnp.cumsum(tallies), jnp.arange(rows * top), side="right").astype(jnp.int32)
    grid = members.reshape(top, rows).T
    grid = grid[jax.random.permutation(jax.random.fold_in(own, 1), rows)]
    offset_by = jax.random.randint(jax.random.fold_in(own, 2), (rows, 1), 0, top)
    return jnp.take_along_axis(grid, (jnp.arange(top)[None, :] + offset_by) % top, axis=1)


def portions_of(amount, total, reach, skew, full):
    weights = [(1 << 20) // math.isqrt(grade ** skew) + 1 for grade in range(1, amount + 1)]
    largest = reach if full else min(reach, max(-(-total // amount), total * weights[0] // sum(weights)))
    least = 1 if total - largest >= amount - 1 else 0
    counts, surplus = [largest] + [least] * (amount - 1), total - largest - least * (amount - 1)
    while surplus > 0:
        candidates = [i for i in range(1, amount) if counts[i] < largest] or [i for i in range(1, amount) if counts[i] < reach]
        whole, remaining = sum([weights[i] for i in candidates]), surplus
        for i in candidates:
            more = min(reach - counts[i], max(1, remaining * weights[i] // whole), surplus)
            counts[i] = counts[i] + more
            surplus = surplus - more
    return np.array(counts)


def centred(own_key, dims, deviation, limit, pieces=(), kind=jnp.bfloat16):
    factor_of = shard_levels(own_key, dims, pieces, -0.22, 0.18) if pieces else 1.0
    drawn = jax.random.normal(own_key, dims, jnp.float32) * deviation * factor_of
    return jnp.minimum(jnp.maximum(drawn, -limit), limit).astype(kind)


def setup_inputs(seed: int = 0) -> dict:
    seeds = jax.random.split(jax.random.key(seed), 7)
    trailing = draw_trailing(jax.random.fold_in(seeds[6], 71), 0)
    panel = centred(seeds[1], (POLES, 2, M, W), (2 * M) ** -0.5, 0.0625, ((0, 4), (2, 8)))
    diag_inverse = centred(seeds[2], (POLES, 2, W, W), 1.0, 6.0, ((0, 4), (2, 8)))
    pole_weights = centred(seeds[3], (POLES, 2), POLES ** -0.5, 3.0, ((0, 4),), jnp.float32)
    owner_map_keys = jax.random.split(jax.random.fold_in(seeds[4], 1), M // RD)
    owner_map_turns = jax.random.permutation(jax.random.fold_in(seeds[4], 3), M // RD)
    owner_map = jax.vmap(lambda own, number: assign_block(jax.random.fold_in(seeds[4], 2), own, number, RD, N_POLE, 1, CAP, 2))(owner_map_keys, owner_map_turns).reshape((M, 1))
    ham_slab = centred(seeds[5], (W, M), W ** -0.5, 0.375)
    return {"trailing": trailing, "panel": panel, "diag_inverse": diag_inverse, "pole_weights": pole_weights, "owner_map": owner_map, "ham_slab": ham_slab}


def batched(form, left, right):
    return jnp.einsum(form, left.astype(jnp.float32), right.astype(jnp.float32))


def reference(trailing, panel, diag_inverse, pole_weights, owner_map, ham_slab):
    grid_real = trailing[:, 0]
    grid_imag = trailing[:, 1]
    low_real = panel[:, 0]
    low_imag = panel[:, 1]
    form = "pmn,pnw->pmw"
    cross_real = -(batched(form, grid_real, low_real) - batched(form, grid_imag, low_imag))
    cross_imag = -(batched(form, grid_real, low_imag) + batched(form, grid_imag, low_real))
    cross_real = cross_real.astype(jnp.bfloat16).astype(jnp.float32)
    cross_imag = cross_imag.astype(jnp.bfloat16).astype(jnp.float32)
    weight_real = pole_weights[:, 0][:, None, None]
    weight_imag = pole_weights[:, 1][:, None, None]
    density_rows = jnp.sum(weight_real * cross_imag + weight_imag * cross_real, axis=0)
    density_half = density_rows.astype(jnp.bfloat16)
    tform = "pmw,pmv->pwv"
    quad_real = batched(tform, low_real, cross_real) - batched(tform, low_imag, cross_imag)
    quad_imag = batched(tform, low_real, cross_imag) + batched(tform, low_imag, cross_real)
    inverse_real = diag_inverse[:, 0].astype(jnp.float32) - quad_real
    inverse_imag = diag_inverse[:, 1].astype(jnp.float32) - quad_imag
    density_diag = jnp.sum(weight_real * inverse_imag + weight_imag * inverse_real, axis=0)
    owners = owner_map[:, 0].astype(jnp.int32)
    positions = lax.broadcasted_iota(jnp.int32, (M,), 0)
    shard = positions // RD
    keyed = shard * N_POLE + owners
    same = keyed[:, None] == keyed[None, :]
    earlier = positions[None, :] < positions[:, None]
    rank = jnp.sum((same & earlier).astype(jnp.int32), axis=1)
    slot = owners * (N_GRID * CAP) + shard * CAP + rank
    patch = jnp.zeros((SLOTS, W), jnp.float32).at[slot].set(density_half.astype(jnp.float32))
    patch = patch.astype(jnp.bfloat16)
    patch_energy = jnp.dot(patch, ham_slab, preferred_element_type=jnp.float32).astype(jnp.bfloat16)
    return (density_diag, patch_energy)
```

```python
import functools

import jax
import jax.numpy as jnp
from jax import lax
from jax.experimental import pallas as pl
from jax.experimental.pallas import tpu as pltpu
from jax.sharding import PartitionSpec as P

MESH = pl.DeviceIdType.MESH
LAG = 2


def complex_product(left_real, left_imag, right_real, right_imag, form):

    def product(first, second):
        return jnp.einsum(form, first, second, preferred_element_type=jnp.float32)

    real = product(left_real, right_real) - product(left_imag, right_imag)
    imag = product(left_real, right_imag) + product(left_imag, right_real)
    return (real, imag)


def per_device_small(trailing, panel, diag_inverse, pole_weights, owner_map, ham_slab):
    rows_here = trailing.shape[2]
    piece = lax.all_gather(panel, "grid", axis=2, tiled=True)
    real, imag = complex_product(
        trailing[:, 0], trailing[:, 1], piece[:, 0], piece[:, 1], "prn,pnw->prw"
    )
    cross_real = (-real).astype(jnp.bfloat16)
    cross_imag = (-imag).astype(jnp.bfloat16)
    weight_real = pole_weights[:, 0][:, None, None]
    weight_imag = pole_weights[:, 1][:, None, None]
    density_rows = jnp.sum(
        weight_real * cross_imag.astype(jnp.float32) + weight_imag * cross_real.astype(jnp.float32),
        axis=0,
    )
    quad_real, quad_imag = complex_product(
        panel[:, 0], panel[:, 1], cross_real, cross_imag, "prw,prv->pwv"
    )
    quad_part = -jnp.sum(weight_real * quad_imag + weight_imag * quad_real, axis=0)
    diag_term = jnp.sum(
        weight_real * diag_inverse[:, 1].astype(jnp.float32)
        + weight_imag * diag_inverse[:, 0].astype(jnp.float32),
        axis=0,
    )
    mine = lax.psum_scatter(quad_part, "grid", scatter_dimension=0, tiled=True) + diag_term
    density_diag = lax.psum(mine, "pole")
    owners = owner_map[:, 0]
    capacity = 2 * rows_here // lax.axis_size("pole")
    same = owners[:, None] == owners[None, :]
    earlier = lax.broadcasted_iota(jnp.int32, (rows_here, rows_here), 1) < lax.broadcasted_iota(
        jnp.int32, (rows_here, rows_here), 0
    )
    rank = jnp.sum((same & earlier).astype(jnp.int32), axis=1)
    slot = owners * capacity + rank
    all_slots = lax.axis_size("pole") * capacity
    placement = (
        slot[:, None] == lax.broadcasted_iota(jnp.int32, (rows_here, all_slots), 1)
    ).astype(jnp.float32)
    total_rows = lax.psum(density_rows, "pole")
    chosen = lax.dynamic_slice_in_dim(placement, lax.axis_index("pole") * capacity, capacity, 1)
    owned_rows = jnp.einsum("rs,rw->sw", chosen, total_rows, precision=lax.Precision.HIGHEST)
    patch = owned_rows.astype(jnp.bfloat16)
    patch_energy = jnp.dot(patch, ham_slab, preferred_element_type=jnp.float32).astype(jnp.bfloat16)
    return (density_diag, patch_energy)


def dot(first, second, over_first=1):
    return lax.dot_general(
        first, second, (((over_first,), (0,)), ((), ())), preferred_element_type=jnp.float32
    )


def kernel(
    n_pole, n_grid, trailing, panel, weights, owners, diag, patch_ref, dd_ref,
    gbuf, lbuf, acc, place, packed, rbuf, qbuf, abuf, sbuf, bbuf, obuf,
    gsem, lsem, fwd_send, fwd_recv, p_send, p_recv, a_send, a_recv, b_send, b_recv, c_send, c_recv,
):
    ny = 2
    nz = n_grid // ny
    rows = gbuf.shape[1]
    half = rows // 2
    cap = rbuf.shape[1]
    sub = obuf.shape[1]
    pole, me = lax.axis_index("pole"), lax.axis_index("grid")
    z, y = me // ny, me % ny

    gcopies = [
        pltpu.make_async_copy(trailing.at[0, c], gbuf.at[c], gsem.at[c]) for c in range(2)
    ]
    lcopies = [
        pltpu.make_async_copy(
            panel.at[0, c, pl.ds(h * half, half)], lbuf.at[me, h, c], lsem.at[2 * h + c]
        )
        for h in range(2)
        for c in range(2)
    ]
    for copy in lcopies + gcopies:
        copy.start()

    barrier = pltpu.get_barrier_semaphore()
    for k in range(1, n_grid):
        pl.semaphore_signal(
            barrier, inc=1, device_id=(pole, lax.rem(me + k, n_grid)), device_id_type=MESH
        )
    for k in range(1, n_pole):
        pl.semaphore_signal(
            barrier, inc=1, device_id=(lax.rem(pole + k, n_pole), me), device_id_type=MESH
        )

    names = lax.broadcasted_iota(jnp.int32, (16, rows), 0) == owners[...]
    ones = names.astype(jnp.float32)
    before = (
        lax.broadcasted_iota(jnp.int32, (rows, rows), 0)
        < lax.broadcasted_iota(jnp.int32, (rows, rows), 1)
    ).astype(jnp.float32)
    counts = dot(ones.astype(jnp.bfloat16), before.astype(jnp.bfloat16))
    rank = jnp.sum(ones * counts, axis=0, keepdims=True).astype(jnp.int32)
    slot = owners[...] * cap + rank
    for q in range(n_pole):
        here = lax.broadcasted_iota(jnp.int32, (cap, rows), 0) + q * cap == slot
        place[q] = here.astype(jnp.float32).astype(jnp.bfloat16)
    acc[...] = jnp.zeros_like(acc)

    for copy in lcopies:
        copy.wait()
    pl.semaphore_wait(barrier, n_grid - 1 + n_pole - 1)

    def sends(kind, d, h, s, src):
        own_line = kind == 0
        first = d == 0
        turn = (kind == 1) & first & (h == 0)
        up = (z + 1 < nz) & ((own_line & (first | (s == -1))) | turn)
        down = (z >= 1) & ((own_line & (first | (s == 1))) | turn)
        over = own_line & jnp.logical_not((d == 1) & (h == 0))
        targets = (jnp.minimum(z + 1, nz - 1) * ny + y, jnp.maximum(z - 1, 0) * ny + y, z * ny + 1 - y)
        out = []
        for j, (cond, target) in enumerate(zip((up, down, over), targets)):
            out.append((cond, pltpu.make_async_remote_copy(
                src_ref=lbuf.at[src, h],
                dst_ref=lbuf.at[src, h],
                send_sem=fwd_send.at[(src * 2 + h) * 3 + j],
                recv_sem=fwd_recv.at[src * 2 + h],
                device_id=(pole, target),
                device_id_type=MESH,
            )))
        return out

    def event(i):
        t, r = i // 4, i % 4
        kind, side = r // 2, r % 2
        tt = jnp.maximum(t - kind * LAG, 0)
        d, h = tt // 2, tt % 2
        s = 1 - 2 * side
        src_z = z + s * d
        valid = (t >= kind * LAG) & (t - kind * LAG < 2 * nz) & (src_z >= 0) & (src_z < nz)
        valid = valid & jnp.logical_not((d == 0) & (side == 1))
        src = jnp.clip(src_z, 0, nz - 1) * ny + jnp.where(kind == 0, y, 1 - y)
        return valid, kind, d, h, s, src

    zero = jnp.int32(0)
    for h in range(2):
        for cond, copy in sends(zero, zero, jnp.int32(h), jnp.int32(1), me):
            pl.when(cond)(copy.start)
    for copy in gcopies:
        copy.wait()

    def step(i, carry):
        valid, kind, d, h, s, src = event(i)

        @pl.when(valid)
        def _():
            @pl.when((d > 0) | (kind == 1))
            def _():
                pltpu.make_async_remote_copy(
                    src_ref=lbuf.at[src, h],
                    dst_ref=lbuf.at[src, h],
                    send_sem=fwd_send.at[(src * 2 + h) * 3],
                    recv_sem=fwd_recv.at[src * 2 + h],
                    device_id=(pole, z * ny + 1 - y),
                    device_id_type=MESH,
                ).wait_recv()
                for cond, copy in sends(kind, d, h, s, src):
                    pl.when(cond)(copy.start)

            cols = pl.ds(pl.multiple_of(src * rows + h * half, half), half)
            g_r, g_i = gbuf[0, :, cols], gbuf[1, :, cols]
            l_r, l_i = lbuf[src, h, 0], lbuf[src, h, 1]
            acc[0] += dot(g_r, l_r) - dot(g_i, l_i)
            acc[1] += dot(g_r, l_i) + dot(g_i, l_r)

        return carry

    lax.fori_loop(0, 4 * (2 * nz + LAG), step, 0)

    w_r, w_i = weights[0, 0], weights[0, 1]
    x_r, x_i = -acc[0], -acc[1]
    dens = (w_r * x_i + w_i * x_r).astype(jnp.bfloat16)
    other = (w_r * x_r - w_i * x_i).astype(jnp.bfloat16)

    p_copies = []
    for k in range(1, n_pole):
        q = lax.rem(pole + k, n_pole)
        packed[k] = dot(place[q], dens).astype(jnp.bfloat16)
        p_copies.append(pltpu.make_async_remote_copy(
            src_ref=packed.at[k], dst_ref=rbuf.at[k - 1],
            send_sem=p_send.at[k - 1], recv_sem=p_recv.at[k - 1],
            device_id=(q, me), device_id_type=MESH,
        ))
        p_copies[-1].start()

    quad = jnp.zeros((qbuf.shape[2], qbuf.shape[2]), jnp.float32)
    for h in range(2):
        part = slice(h * half, (h + 1) * half)
        quad += dot(lbuf[me, h, 0], dens[part], 0) + dot(lbuf[me, h, 1], other[part], 0)
    term = w_r * diag[0, 1].astype(jnp.float32) + w_i * diag[0, 0].astype(jnp.float32)
    for p in range(n_pole):
        for g in range(n_grid):
            at = (g * n_pole + p) * sub
            qbuf[p, g * sub:(g + 1) * sub] = -quad[at:at + sub]
        mine = pl.ds(pl.multiple_of(me * sub, sub), sub)
        qbuf[p, mine] += term[p * sub:(p + 1) * sub]
    a_copies = []
    for k in range(1, n_pole):
        q = lax.rem(pole + k, n_pole)
        a_copies.append(pltpu.make_async_remote_copy(
            src_ref=qbuf.at[q], dst_ref=abuf.at[k - 1],
            send_sem=a_send.at[k - 1], recv_sem=a_recv.at[k - 1],
            device_id=(q, me), device_id_type=MESH,
        ))
        a_copies[-1].start()

    owned = dot(place[pole], dens)

    total = qbuf[pole]
    for k in range(1, n_pole):
        a_copies[k - 1].wait_recv()
        total += abuf[k - 1]
    for g in range(n_grid):
        sbuf[g] = total[g * sub:(g + 1) * sub]
    b_copies = []
    for k in range(1, n_grid):
        g = lax.rem(me + k, n_grid)
        b_copies.append(pltpu.make_async_remote_copy(
            src_ref=sbuf.at[g], dst_ref=bbuf.at[k - 1],
            send_sem=b_send.at[k - 1], recv_sem=b_recv.at[k - 1],
            device_id=(pole, g), device_id_type=MESH,
        ))
        b_copies[-1].start()

    for k in range(1, n_pole):
        p_copies[k - 1].wait_recv()
        owned += rbuf[k - 1].astype(jnp.float32)
    patch_ref[...] = owned.astype(jnp.bfloat16)

    final = sbuf[me]
    for k in range(1, n_grid):
        b_copies[k - 1].wait_recv()
        final += bbuf[k - 1]
    obuf[pole] = final
    c_copies = []
    for k in range(1, n_pole):
        q = lax.rem(pole + k, n_pole)
        c_copies.append(pltpu.make_async_remote_copy(
            src_ref=obuf.at[pole], dst_ref=obuf.at[pole],
            send_sem=c_send.at[k - 1], recv_sem=c_recv.at[k - 1],
            device_id=(q, me), device_id_type=MESH,
        ))
        c_copies[-1].start()

    def drain(i, carry):
        valid, kind, d, h, s, src = event(i)
        for cond, copy in sends(kind, d, h, s, src):
            pl.when(valid & cond)(copy.wait_send)
        return carry

    lax.fori_loop(0, 4 * (2 * nz + LAG), drain, 0)
    for copy in p_copies + a_copies + b_copies:
        copy.wait_send()
    for k in range(1, n_pole):
        c_copies[k - 1].wait()
    for p in range(n_pole):
        dd_ref[p * sub:(p + 1) * sub] = obuf[p]


def per_device(n_pole, n_grid, trailing, panel, diag_inverse, pole_weights, owner_map, ham_slab):
    rows, m = trailing.shape[2:]
    w = panel.shape[3]
    half = rows // 2
    cap = 2 * rows // n_pole
    sub = w // n_grid // n_pole
    vmem = pl.BlockSpec(memory_space=pltpu.VMEM)
    dma = pltpu.SemaphoreType.DMA
    patch, density_diag = pl.pallas_call(
        functools.partial(kernel, n_pole, n_grid),
        out_shape=(
            jax.ShapeDtypeStruct((cap, w), jnp.bfloat16),
            jax.ShapeDtypeStruct((w // n_grid, w), jnp.float32),
        ),
        in_specs=[
            pl.BlockSpec(memory_space=pl.ANY),
            pl.BlockSpec(memory_space=pl.ANY),
            pl.BlockSpec(memory_space=pltpu.SMEM),
            vmem,
            vmem,
        ],
        out_specs=(vmem, vmem),
        scratch_shapes=[
            pltpu.VMEM((2, rows, m), jnp.bfloat16),
            pltpu.VMEM((n_grid, 2, 2, half, w), jnp.bfloat16),
            pltpu.VMEM((2, rows, w), jnp.float32),
            pltpu.VMEM((n_pole, cap, rows), jnp.bfloat16),
            pltpu.VMEM((n_pole, cap, w), jnp.bfloat16),
            pltpu.VMEM((n_pole - 1, cap, w), jnp.bfloat16),
            pltpu.VMEM((n_pole, n_grid * sub, w), jnp.float32),
            pltpu.VMEM((n_pole - 1, n_grid * sub, w), jnp.float32),
            pltpu.VMEM((n_grid, sub, w), jnp.float32),
            pltpu.VMEM((n_grid - 1, sub, w), jnp.float32),
            pltpu.VMEM((n_pole, sub, w), jnp.float32),
            dma((2,)),
            dma((4,)),
            dma((n_grid * 6,)),
            dma((n_grid * 2,)),
            dma((n_pole - 1,)),
            dma((n_pole - 1,)),
            dma((n_pole - 1,)),
            dma((n_pole - 1,)),
            dma((n_grid - 1,)),
            dma((n_grid - 1,)),
            dma((n_pole - 1,)),
            dma((n_pole - 1,)),
        ],
        compiler_params=pltpu.CompilerParams(
            collective_id=0, has_side_effects=True, vmem_limit_bytes=40 * 1024 * 1024
        ),
        cost_estimate=pl.CostEstimate(
            flops=8 * rows * m * w, bytes_accessed=4 * rows * m, transcendentals=0
        ),
    )(trailing, panel, pole_weights, owner_map.reshape(1, rows), diag_inverse)
    patch_energy = jnp.dot(patch, ham_slab, preferred_element_type=jnp.float32).astype(jnp.bfloat16)
    return (density_diag, patch_energy)


def solution(mesh):
    n_pole, n_grid = mesh.shape["pole"], mesh.shape["grid"]
    placed = (
        P("pole", None, "grid", None),
        P("pole", None, "grid", None),
        P("pole", None, "grid", None),
        P("pole", None),
        P("grid", None),
        P(),
    )

    def body(trailing, panel, *rest):
        rows, w = panel.shape[2:]
        fits = (
            panel.shape[0] == 1
            and n_pole <= 16
            and n_grid % 2 == 0
            and rows % 256 == 0
            and (2 * rows // n_pole) % 16 == 0
            and w % (8 * n_grid * n_pole) == 0
            and w % 128 == 0
        )
        if fits:
            return per_device(n_pole, n_grid, trailing, panel, *rest)
        return per_device_small(trailing, panel, *rest)

    return jax.shard_map(
        body,
        mesh=mesh,
        in_specs=placed,
        out_specs=(P("grid", None), P(("pole", "grid"), None)),
        check_vma=False,
    )
```

```python
import functools

import jax
import jax.numpy as jnp
from jax import lax
from jax.experimental import pallas as pl
from jax.experimental.pallas import tpu as pltpu
from jax.sharding import PartitionSpec as P

MESH = pl.DeviceIdType.MESH
LAG = 2


def complex_product(left_real, left_imag, right_real, right_imag, form):

    def product(first, second):
        return jnp.einsum(form, first, second, preferred_element_type=jnp.float32)

    real = product(left_real, right_real) - product(left_imag, right_imag)
    imag = product(left_real, right_imag) + product(left_imag, right_real)
    return (real, imag)


def per_device_small(trailing, panel, diag_inverse, pole_weights, owner_map, ham_slab):
    rows_here = trailing.shape[2]
    piece = lax.all_gather(panel, "grid", axis=2, tiled=True)
    real, imag = complex_product(
        trailing[:, 0], trailing[:, 1], piece[:, 0], piece[:, 1], "prn,pnw->prw"
    )
    cross_real = (-real).astype(jnp.bfloat16)
    cross_imag = (-imag).astype(jnp.bfloat16)
    weight_real = pole_weights[:, 0][:, None, None]
    weight_imag = pole_weights[:, 1][:, None, None]
    density_rows = jnp.sum(
        weight_real * cross_imag.astype(jnp.float32) + weight_imag * cross_real.astype(jnp.float32),
        axis=0,
    )
    quad_real, quad_imag = complex_product(
        panel[:, 0], panel[:, 1], cross_real, cross_imag, "prw,prv->pwv"
    )
    quad_part = -jnp.sum(weight_real * quad_imag + weight_imag * quad_real, axis=0)
    diag_term = jnp.sum(
        weight_real * diag_inverse[:, 1].astype(jnp.float32)
        + weight_imag * diag_inverse[:, 0].astype(jnp.float32),
        axis=0,
    )
    mine = lax.psum_scatter(quad_part, "grid", scatter_dimension=0, tiled=True) + diag_term
    density_diag = lax.psum(mine, "pole")
    owners = owner_map[:, 0]
    capacity = 2 * rows_here // lax.axis_size("pole")
    same = owners[:, None] == owners[None, :]
    earlier = lax.broadcasted_iota(jnp.int32, (rows_here, rows_here), 1) < lax.broadcasted_iota(
        jnp.int32, (rows_here, rows_here), 0
    )
    rank = jnp.sum((same & earlier).astype(jnp.int32), axis=1)
    slot = owners * capacity + rank
    all_slots = lax.axis_size("pole") * capacity
    placement = (
        slot[:, None] == lax.broadcasted_iota(jnp.int32, (rows_here, all_slots), 1)
    ).astype(jnp.float32)
    total_rows = lax.psum(density_rows, "pole")
    chosen = lax.dynamic_slice_in_dim(placement, lax.axis_index("pole") * capacity, capacity, 1)
    owned_rows = jnp.einsum("rs,rw->sw", chosen, total_rows, precision=lax.Precision.HIGHEST)
    patch = owned_rows.astype(jnp.bfloat16)
    patch_energy = jnp.dot(patch, ham_slab, preferred_element_type=jnp.float32).astype(jnp.bfloat16)
    return (density_diag, patch_energy)


def dot(first, second, over_first=1):
    return lax.dot_general(
        first, second, (((over_first,), (0,)), ((), ())), preferred_element_type=jnp.float32
    )


def kernel(
    n_pole, n_grid, trailing, panel, weights, owners, diag, patch_ref, dd_ref,
    gbuf, lbuf, acc, place, packed, mbuf, sums, pbuf, rbuf, qbuf, abuf, bbuf, obuf,
    gsem, lsem, fwd_send, fwd_recv, m_sem, p_send, p_recv, a_send, a_recv, c_send, c_recv,
):
    ny = 2
    nz = n_grid // ny
    rows = gbuf.shape[1]
    half = rows // 2
    cap = rbuf.shape[1]
    sub, w = obuf.shape[1:]
    pole, me = lax.axis_index("pole"), lax.axis_index("grid")
    z, y = me // ny, me % ny

    gcopies = [
        pltpu.make_async_copy(trailing.at[0, c], gbuf.at[c], gsem.at[c]) for c in range(2)
    ]
    lcopies = [
        pltpu.make_async_copy(
            panel.at[0, c, pl.ds(h * half, half)], lbuf.at[me, h, c], lsem.at[2 * h + c]
        )
        for h in range(2)
        for c in range(2)
    ]
    for copy in lcopies + gcopies:
        copy.start()

    barrier = pltpu.get_barrier_semaphore()
    for k in range(1, n_grid):
        pl.semaphore_signal(
            barrier, inc=1, device_id=(pole, lax.rem(me + k, n_grid)), device_id_type=MESH
        )
    for k in range(1, n_pole):
        pl.semaphore_signal(
            barrier, inc=1, device_id=(lax.rem(pole + k, n_pole), me), device_id_type=MESH
        )

    names = lax.broadcasted_iota(jnp.int32, (16, rows), 0) == owners[...]
    ones = names.astype(jnp.float32)
    before = (
        lax.broadcasted_iota(jnp.int32, (rows, rows), 0)
        < lax.broadcasted_iota(jnp.int32, (rows, rows), 1)
    ).astype(jnp.float32)
    counts = dot(ones.astype(jnp.bfloat16), before.astype(jnp.bfloat16))
    rank = jnp.sum(ones * counts, axis=0, keepdims=True).astype(jnp.int32)
    slot = owners[...] * cap + rank
    for q in range(n_pole):
        here = lax.broadcasted_iota(jnp.int32, (cap, rows), 0) + q * cap == slot
        place[q] = here.astype(jnp.float32).astype(jnp.bfloat16)
    acc[...] = jnp.zeros_like(acc)

    for copy in lcopies:
        copy.wait()
    pl.semaphore_wait(barrier, n_grid - 1 + n_pole - 1)

    def sends(kind, d, h, s, src):
        own_line = kind == 0
        first = d == 0
        turn = (kind == 1) & first & (h == 0)
        up = (z + 1 < nz) & ((own_line & (first | (s == -1))) | turn)
        down = (z >= 1) & ((own_line & (first | (s == 1))) | turn)
        over = own_line & jnp.logical_not((d == 1) & (h == 0))
        targets = (jnp.minimum(z + 1, nz - 1) * ny + y, jnp.maximum(z - 1, 0) * ny + y, z * ny + 1 - y)
        out = []
        for j, (cond, target) in enumerate(zip((up, down, over), targets)):
            out.append((cond, pltpu.make_async_remote_copy(
                src_ref=lbuf.at[src, h],
                dst_ref=lbuf.at[src, h],
                send_sem=fwd_send.at[(src * 2 + h) * 3 + j],
                recv_sem=fwd_recv.at[src * 2 + h],
                device_id=(pole, target),
                device_id_type=MESH,
            )))
        return out

    def event(i):
        t, r = i // 4, i % 4
        kind, side = r // 2, r % 2
        tt = jnp.maximum(t - kind * LAG, 0)
        d, h = tt // 2, tt % 2
        s = 1 - 2 * side
        src_z = z + s * d
        valid = (t >= kind * LAG) & (t - kind * LAG < 2 * nz) & (src_z >= 0) & (src_z < nz)
        valid = valid & jnp.logical_not((d == 0) & (side == 1))
        src = jnp.clip(src_z, 0, nz - 1) * ny + jnp.where(kind == 0, y, 1 - y)
        return valid, kind, d, h, s, src

    zero = jnp.int32(0)
    for h in range(2):
        for cond, copy in sends(zero, zero, jnp.int32(h), jnp.int32(1), me):
            pl.when(cond)(copy.start)
    for copy in gcopies:
        copy.wait()

    def step(i, carry):
        valid, kind, d, h, s, src = event(i)

        @pl.when(valid)
        def _():
            @pl.when((d > 0) | (kind == 1))
            def _():
                pltpu.make_async_remote_copy(
                    src_ref=lbuf.at[src, h],
                    dst_ref=lbuf.at[src, h],
                    send_sem=fwd_send.at[(src * 2 + h) * 3],
                    recv_sem=fwd_recv.at[src * 2 + h],
                    device_id=(pole, z * ny + 1 - y),
                    device_id_type=MESH,
                ).wait_recv()
                for cond, copy in sends(kind, d, h, s, src):
                    pl.when(cond)(copy.start)

            cols = pl.ds(pl.multiple_of(src * rows + h * half, half), half)
            g_r, g_i = gbuf[0, :, cols], gbuf[1, :, cols]
            l_r, l_i = lbuf[src, h, 0], lbuf[src, h, 1]
            acc[0] += dot(g_r, l_r) - dot(g_i, l_i)
            acc[1] += dot(g_r, l_i) + dot(g_i, l_r)

        return carry

    lax.fori_loop(0, 4 * (2 * nz + LAG), step, 0)

    w_r, w_i = weights[0, 0], weights[0, 1]
    x_r, x_i = -acc[0], -acc[1]
    dens = (w_r * x_i + w_i * x_r).astype(jnp.bfloat16)
    other = (w_r * x_r - w_i * x_i).astype(jnp.bfloat16)

    core, cap_sets = pole % 2, n_pole // 2
    mate = pole + 1 - 2 * core
    for j in range(cap_sets):
        packed[j] = dot(place[2 * j + 1 - core], dens).astype(jnp.bfloat16)
    mate_copy = pltpu.make_async_remote_copy(
        src_ref=packed, dst_ref=mbuf, send_sem=m_sem.at[0], recv_sem=m_sem.at[1],
        device_id=(mate, me), device_id_type=MESH,
    )
    mate_copy.start()

    quad = jnp.zeros((w, w), jnp.float32)
    for h in range(2):
        part = slice(h * half, (h + 1) * half)
        quad += dot(lbuf[me, h, 0], dens[part], 0) + dot(lbuf[me, h, 1], other[part], 0)
    qbuf[...] = -quad
    for g in range(n_grid):
        abuf[g] = qbuf[g * sub:(g + 1) * sub].astype(jnp.bfloat16)
    a_copies = []
    for k in range(1, n_grid):
        g = lax.rem(me + k, n_grid)
        a_copies.append(pltpu.make_async_remote_copy(
            src_ref=abuf.at[g], dst_ref=bbuf.at[k - 1],
            send_sem=a_send.at[k - 1], recv_sem=a_recv.at[k - 1],
            device_id=(pole, g), device_id_type=MESH,
        ))
        a_copies[-1].start()
    term = w_r * diag[0, 1].astype(jnp.float32) + w_i * diag[0, 0].astype(jnp.float32)
    final = term + qbuf[pl.ds(pl.multiple_of(me * sub, sub), sub)]
    for j in range(cap_sets):
        sums[j] = dot(place[2 * j + core], dens)

    mate_copy.wait_recv()
    p_copies = []
    for k in range(1, cap_sets):
        j = lax.rem(pole // 2 + k, cap_sets)
        pbuf[k - 1] = (sums[j] + mbuf[j].astype(jnp.float32)).astype(jnp.bfloat16)
        p_copies.append(pltpu.make_async_remote_copy(
            src_ref=pbuf.at[k - 1], dst_ref=rbuf.at[k - 1],
            send_sem=p_send.at[k - 1], recv_sem=p_recv.at[k - 1],
            device_id=(2 * j + core, me), device_id_type=MESH,
        ))
        p_copies[-1].start()
    owned = sums[pole // 2] + mbuf[pole // 2].astype(jnp.float32)

    for k in range(1, n_grid):
        a_copies[k - 1].wait_recv()
        final += bbuf[k - 1].astype(jnp.float32)
    obuf[pole] = final
    c_copies = []
    for k in range(1, n_pole):
        c_copies.append(pltpu.make_async_remote_copy(
            src_ref=obuf.at[pole], dst_ref=obuf.at[pole],
            send_sem=c_send.at[k - 1], recv_sem=c_recv.at[k - 1],
            device_id=(lax.rem(pole + k, n_pole), me), device_id_type=MESH,
        ))
        c_copies[-1].start()

    def drain(i, carry):
        valid, kind, d, h, s, src = event(i)
        for cond, copy in sends(kind, d, h, s, src):
            pl.when(valid & cond)(copy.wait_send)
        return carry

    lax.fori_loop(0, 4 * (2 * nz + LAG), drain, 0)
    mate_copy.wait_send()
    for copy in p_copies:
        copy.wait()
    for k in range(1, cap_sets):
        owned += rbuf[k - 1].astype(jnp.float32)
    patch_ref[...] = owned.astype(jnp.bfloat16)
    for copy in a_copies:
        copy.wait_send()
    for k in range(1, n_pole):
        c_copies[k - 1].wait()
    result = obuf[0]
    for p in range(1, n_pole):
        result += obuf[p]
    dd_ref[...] = result


def per_device(n_pole, n_grid, trailing, panel, diag_inverse, pole_weights, owner_map, ham_slab):
    rows, m = trailing.shape[2:]
    w = panel.shape[3]
    half = rows // 2
    cap = 2 * rows // n_pole
    sub = w // n_grid
    vmem = pl.BlockSpec(memory_space=pltpu.VMEM)
    dma = pltpu.SemaphoreType.DMA
    patch, density_diag = pl.pallas_call(
        functools.partial(kernel, n_pole, n_grid),
        out_shape=(
            jax.ShapeDtypeStruct((cap, w), jnp.bfloat16),
            jax.ShapeDtypeStruct((w // n_grid, w), jnp.float32),
        ),
        in_specs=[
            pl.BlockSpec(memory_space=pl.ANY),
            pl.BlockSpec(memory_space=pl.ANY),
            pl.BlockSpec(memory_space=pltpu.SMEM),
            vmem,
            vmem,
        ],
        out_specs=(vmem, vmem),
        scratch_shapes=[
            pltpu.VMEM((2, rows, m), jnp.bfloat16),
            pltpu.VMEM((n_grid, 2, 2, half, w), jnp.bfloat16),
            pltpu.VMEM((2, rows, w), jnp.float32),
            pltpu.VMEM((n_pole, cap, rows), jnp.bfloat16),
            pltpu.VMEM((n_pole // 2, cap, w), jnp.bfloat16),
            pltpu.VMEM((n_pole // 2, cap, w), jnp.bfloat16),
            pltpu.VMEM((n_pole // 2, cap, w), jnp.float32),
            pltpu.VMEM((n_pole // 2 - 1, cap, w), jnp.bfloat16),
            pltpu.VMEM((n_pole // 2 - 1, cap, w), jnp.bfloat16),
            pltpu.VMEM((w, w), jnp.float32),
            pltpu.VMEM((n_grid, sub, w), jnp.bfloat16),
            pltpu.VMEM((n_grid - 1, sub, w), jnp.bfloat16),
            pltpu.VMEM((n_pole, sub, w), jnp.float32),
            dma((2,)),
            dma((4,)),
            dma((n_grid * 6,)),
            dma((n_grid * 2,)),
            dma((2,)),
            dma((n_pole // 2 - 1,)),
            dma((n_pole // 2 - 1,)),
            dma((n_grid - 1,)),
            dma((n_grid - 1,)),
            dma((n_pole - 1,)),
            dma((n_pole - 1,)),
        ],
        compiler_params=pltpu.CompilerParams(
            collective_id=0, has_side_effects=True, vmem_limit_bytes=60 * 1024 * 1024
        ),
        cost_estimate=pl.CostEstimate(
            flops=8 * rows * m * w, bytes_accessed=4 * rows * m, transcendentals=0
        ),
    )(trailing, panel, pole_weights, owner_map.reshape(1, rows), diag_inverse)
    patch_energy = jnp.dot(patch, ham_slab, preferred_element_type=jnp.float32).astype(jnp.bfloat16)
    return (density_diag, patch_energy)


def solution(mesh):
    n_pole, n_grid = mesh.shape["pole"], mesh.shape["grid"]
    placed = (
        P("pole", None, "grid", None),
        P("pole", None, "grid", None),
        P("pole", None, "grid", None),
        P("pole", None),
        P("grid", None),
        P(),
    )

    def body(trailing, panel, *rest):
        rows, w = panel.shape[2:]
        fits = (
            panel.shape[0] == 1
            and n_pole % 2 == 0
            and 4 <= n_pole <= 16
            and n_grid % 2 == 0
            and rows % 256 == 0
            and (2 * rows // n_pole) % 16 == 0
            and w % (16 * n_grid) == 0
            and w % 128 == 0
        )
        if fits:
            return per_device(n_pole, n_grid, trailing, panel, *rest)
        return per_device_small(trailing, panel, *rest)

    return jax.shard_map(
        body,
        mesh=mesh,
        in_specs=placed,
        out_specs=(P("grid", None), P(("pole", "grid"), None)),
        check_vma=False,
    )
```

```python
import functools

import jax
import jax.numpy as jnp
from jax import lax
from jax.experimental import pallas as pl
from jax.experimental.pallas import tpu as pltpu
from jax.sharding import PartitionSpec as P

MESH = pl.DeviceIdType.MESH
LAG = 2


def complex_product(left_real, left_imag, right_real, right_imag, form):

    def product(first, second):
        return jnp.einsum(form, first, second, preferred_element_type=jnp.float32)

    real = product(left_real, right_real) - product(left_imag, right_imag)
    imag = product(left_real, right_imag) + product(left_imag, right_real)
    return (real, imag)


def per_device_small(trailing, panel, diag_inverse, pole_weights, owner_map, ham_slab):
    rows_here = trailing.shape[2]
    piece = lax.all_gather(panel, "grid", axis=2, tiled=True)
    real, imag = complex_product(
        trailing[:, 0], trailing[:, 1], piece[:, 0], piece[:, 1], "prn,pnw->prw"
    )
    cross_real = (-real).astype(jnp.bfloat16)
    cross_imag = (-imag).astype(jnp.bfloat16)
    weight_real = pole_weights[:, 0][:, None, None]
    weight_imag = pole_weights[:, 1][:, None, None]
    density_rows = jnp.sum(
        weight_real * cross_imag.astype(jnp.float32) + weight_imag * cross_real.astype(jnp.float32),
        axis=0,
    )
    quad_real, quad_imag = complex_product(
        panel[:, 0], panel[:, 1], cross_real, cross_imag, "prw,prv->pwv"
    )
    quad_part = -jnp.sum(weight_real * quad_imag + weight_imag * quad_real, axis=0)
    diag_term = jnp.sum(
        weight_real * diag_inverse[:, 1].astype(jnp.float32)
        + weight_imag * diag_inverse[:, 0].astype(jnp.float32),
        axis=0,
    )
    mine = lax.psum_scatter(quad_part, "grid", scatter_dimension=0, tiled=True) + diag_term
    density_diag = lax.psum(mine, "pole")
    owners = owner_map[:, 0]
    capacity = 2 * rows_here // lax.axis_size("pole")
    same = owners[:, None] == owners[None, :]
    earlier = lax.broadcasted_iota(jnp.int32, (rows_here, rows_here), 1) < lax.broadcasted_iota(
        jnp.int32, (rows_here, rows_here), 0
    )
    rank = jnp.sum((same & earlier).astype(jnp.int32), axis=1)
    slot = owners * capacity + rank
    all_slots = lax.axis_size("pole") * capacity
    placement = (
        slot[:, None] == lax.broadcasted_iota(jnp.int32, (rows_here, all_slots), 1)
    ).astype(jnp.float32)
    total_rows = lax.psum(density_rows, "pole")
    chosen = lax.dynamic_slice_in_dim(placement, lax.axis_index("pole") * capacity, capacity, 1)
    owned_rows = jnp.einsum("rs,rw->sw", chosen, total_rows, precision=lax.Precision.HIGHEST)
    patch = owned_rows.astype(jnp.bfloat16)
    patch_energy = jnp.dot(patch, ham_slab, preferred_element_type=jnp.float32).astype(jnp.bfloat16)
    return (density_diag, patch_energy)


def dot(first, second, over_first=1):
    return lax.dot_general(
        first, second, (((over_first,), (0,)), ((), ())), preferred_element_type=jnp.float32
    )


def kernel(
    n_pole, n_grid, trailing, panel, weights, owners, diag, patch_ref, dd_ref,
    gbuf, lbuf, acc, place, packed, mbuf, sums, pbuf, rbuf, qbuf, abuf, bbuf, obuf,
    gsem, lsem, fwd_send, fwd_recv, m_sem, p_send, p_recv, a_send, a_recv, c_send, c_recv,
):
    ny = 2
    nz = n_grid // ny
    rows = gbuf.shape[1]
    half = rows // 2
    cap = rbuf.shape[1]
    sub, w = obuf.shape[1:]
    pole, me = lax.axis_index("pole"), lax.axis_index("grid")
    z, y = me // ny, me % ny

    gcopies = [
        pltpu.make_async_copy(trailing.at[0, c], gbuf.at[c], gsem.at[c]) for c in range(2)
    ]
    lcopies = [
        pltpu.make_async_copy(
            panel.at[0, c, pl.ds(h * half, half)], lbuf.at[me, h, c], lsem.at[2 * h + c]
        )
        for h in range(2)
        for c in range(2)
    ]
    for copy in lcopies + gcopies:
        copy.start()

    barrier = pltpu.get_barrier_semaphore()
    for k in range(1, n_grid):
        pl.semaphore_signal(
            barrier, inc=1, device_id=(pole, lax.rem(me + k, n_grid)), device_id_type=MESH
        )
    for k in range(1, n_pole):
        pl.semaphore_signal(
            barrier, inc=1, device_id=(lax.rem(pole + k, n_pole), me), device_id_type=MESH
        )

    names = lax.broadcasted_iota(jnp.int32, (16, rows), 0) == owners[...]
    ones = names.astype(jnp.float32)
    before = (
        lax.broadcasted_iota(jnp.int32, (rows, rows), 0)
        < lax.broadcasted_iota(jnp.int32, (rows, rows), 1)
    ).astype(jnp.float32)
    counts = dot(ones.astype(jnp.bfloat16), before.astype(jnp.bfloat16))
    rank = jnp.sum(ones * counts, axis=0, keepdims=True).astype(jnp.int32)
    slot = owners[...] * cap + rank
    for q in range(n_pole):
        here = lax.broadcasted_iota(jnp.int32, (cap, rows), 0) + q * cap == slot
        place[q] = here.astype(jnp.float32).astype(jnp.bfloat16)
    acc[...] = jnp.zeros_like(acc)

    for copy in lcopies:
        copy.wait()
    pl.semaphore_wait(barrier, n_grid - 1 + n_pole - 1)

    def sends(kind, d, h, s, src):
        own_line = kind == 0
        first = d == 0
        src_z = src // ny
        turn = (kind == 1) & (h == 0)
        turn_up = turn & jnp.where(z + 1 == nz - 1, src_z == 0, first)
        turn_down = turn & jnp.where(z == 1, src_z == nz - 1, first)
        up = (z + 1 < nz) & ((own_line & (first | (s == -1))) | turn_up)
        down = (z >= 1) & ((own_line & (first | (s == 1))) | turn_down)
        spared = jnp.where((z == 0) | (z == nz - 1), nz - 1, 1)
        over = own_line & jnp.logical_not((d == spared) & (h == 0))
        targets = (jnp.minimum(z + 1, nz - 1) * ny + y, jnp.maximum(z - 1, 0) * ny + y, z * ny + 1 - y)
        out = []
        for j, (cond, target) in enumerate(zip((up, down, over), targets)):
            out.append((cond, pltpu.make_async_remote_copy(
                src_ref=lbuf.at[src, h],
                dst_ref=lbuf.at[src, h],
                send_sem=fwd_send.at[(src * 2 + h) * 3 + j],
                recv_sem=fwd_recv.at[src * 2 + h],
                device_id=(pole, target),
                device_id_type=MESH,
            )))
        return out

    def event(i):
        t, r = i // 4, i % 4
        kind, side = r // 2, r % 2
        tt = jnp.maximum(t - kind * LAG, 0)
        d, h = tt // 2, tt % 2
        s = 1 - 2 * side
        src_z = z + s * d
        valid = (t >= kind * LAG) & (t - kind * LAG < 2 * nz) & (src_z >= 0) & (src_z < nz)
        valid = valid & jnp.logical_not((d == 0) & (side == 1))
        src = jnp.clip(src_z, 0, nz - 1) * ny + jnp.where(kind == 0, y, 1 - y)
        return valid, kind, d, h, s, src

    zero = jnp.int32(0)
    for h in range(2):
        for cond, copy in sends(zero, zero, jnp.int32(h), jnp.int32(1), me):
            pl.when(cond)(copy.start)
    for copy in gcopies:
        copy.wait()

    def step(i, carry):
        valid, kind, d, h, s, src = event(i)

        @pl.when(valid)
        def _():
            @pl.when((d > 0) | (kind == 1))
            def _():
                pltpu.make_async_remote_copy(
                    src_ref=lbuf.at[src, h],
                    dst_ref=lbuf.at[src, h],
                    send_sem=fwd_send.at[(src * 2 + h) * 3],
                    recv_sem=fwd_recv.at[src * 2 + h],
                    device_id=(pole, z * ny + 1 - y),
                    device_id_type=MESH,
                ).wait_recv()
                for cond, copy in sends(kind, d, h, s, src):
                    pl.when(cond)(copy.start)

            cols = pl.ds(pl.multiple_of(src * rows + h * half, half), half)
            g_r, g_i = gbuf[0, :, cols], gbuf[1, :, cols]
            l_r, l_i = lbuf[src, h, 0], lbuf[src, h, 1]
            acc[0] += dot(g_r, l_r) - dot(g_i, l_i)
            acc[1] += dot(g_r, l_i) + dot(g_i, l_r)

        return carry

    lax.fori_loop(0, 4 * (2 * nz + LAG), step, 0)

    w_r, w_i = weights[0, 0], weights[0, 1]
    x_r, x_i = -acc[0], -acc[1]
    dens = (w_r * x_i + w_i * x_r).astype(jnp.bfloat16)
    other = (w_r * x_r - w_i * x_i).astype(jnp.bfloat16)

    core, cap_sets = pole % 2, n_pole // 2
    mate = pole + 1 - 2 * core
    for j in range(cap_sets):
        packed[j] = dot(place[2 * j + 1 - core], dens).astype(jnp.bfloat16)
    mate_copy = pltpu.make_async_remote_copy(
        src_ref=packed, dst_ref=mbuf, send_sem=m_sem.at[0], recv_sem=m_sem.at[1],
        device_id=(mate, me), device_id_type=MESH,
    )
    mate_copy.start()

    quad = jnp.zeros((w, w), jnp.float32)
    for h in range(2):
        part = slice(h * half, (h + 1) * half)
        quad += dot(lbuf[me, h, 0], dens[part], 0) + dot(lbuf[me, h, 1], other[part], 0)
    qbuf[...] = -quad
    for g in range(n_grid):
        abuf[g] = qbuf[g * sub:(g + 1) * sub].astype(jnp.bfloat16)
    a_copies = []
    for k in range(1, n_grid):
        g = lax.rem(me + k, n_grid)
        a_copies.append(pltpu.make_async_remote_copy(
            src_ref=abuf.at[g], dst_ref=bbuf.at[k - 1],
            send_sem=a_send.at[k - 1], recv_sem=a_recv.at[k - 1],
            device_id=(pole, g), device_id_type=MESH,
        ))
        a_copies[-1].start()
    term = w_r * diag[0, 1].astype(jnp.float32) + w_i * diag[0, 0].astype(jnp.float32)
    final = term + qbuf[pl.ds(pl.multiple_of(me * sub, sub), sub)]
    for j in range(cap_sets):
        sums[j] = dot(place[2 * j + core], dens)

    mate_copy.wait_recv()
    p_copies = []
    for k in range(1, cap_sets):
        j = lax.rem(pole // 2 + k, cap_sets)
        pbuf[k - 1] = (sums[j] + mbuf[j].astype(jnp.float32)).astype(jnp.bfloat16)
        p_copies.append(pltpu.make_async_remote_copy(
            src_ref=pbuf.at[k - 1], dst_ref=rbuf.at[k - 1],
            send_sem=p_send.at[k - 1], recv_sem=p_recv.at[k - 1],
            device_id=(2 * j + core, me), device_id_type=MESH,
        ))
        p_copies[-1].start()
    owned = sums[pole // 2] + mbuf[pole // 2].astype(jnp.float32)

    for k in range(1, n_grid):
        a_copies[k - 1].wait_recv()
        final += bbuf[k - 1].astype(jnp.float32)
    obuf[pole] = final
    c_copies = []
    for k in range(1, n_pole):
        c_copies.append(pltpu.make_async_remote_copy(
            src_ref=obuf.at[pole], dst_ref=obuf.at[pole],
            send_sem=c_send.at[k - 1], recv_sem=c_recv.at[k - 1],
            device_id=(lax.rem(pole + k, n_pole), me), device_id_type=MESH,
        ))
        c_copies[-1].start()

    def drain(i, carry):
        valid, kind, d, h, s, src = event(i)
        for cond, copy in sends(kind, d, h, s, src):
            pl.when(valid & cond)(copy.wait_send)
        return carry

    lax.fori_loop(0, 4 * (2 * nz + LAG), drain, 0)
    mate_copy.wait_send()
    for copy in p_copies:
        copy.wait()
    for k in range(1, cap_sets):
        owned += rbuf[k - 1].astype(jnp.float32)
    patch_ref[...] = owned.astype(jnp.bfloat16)
    for copy in a_copies:
        copy.wait_send()
    for k in range(1, n_pole):
        c_copies[k - 1].wait()
    result = obuf[0]
    for p in range(1, n_pole):
        result += obuf[p]
    dd_ref[...] = result


def per_device(n_pole, n_grid, trailing, panel, diag_inverse, pole_weights, owner_map, ham_slab):
    rows, m = trailing.shape[2:]
    w = panel.shape[3]
    half = rows // 2
    cap = 2 * rows // n_pole
    sub = w // n_grid
    vmem = pl.BlockSpec(memory_space=pltpu.VMEM)
    dma = pltpu.SemaphoreType.DMA
    patch, density_diag = pl.pallas_call(
        functools.partial(kernel, n_pole, n_grid),
        out_shape=(
            jax.ShapeDtypeStruct((cap, w), jnp.bfloat16),
            jax.ShapeDtypeStruct((w // n_grid, w), jnp.float32),
        ),
        in_specs=[
            pl.BlockSpec(memory_space=pl.ANY),
            pl.BlockSpec(memory_space=pl.ANY),
            pl.BlockSpec(memory_space=pltpu.SMEM),
            vmem,
            vmem,
        ],
        out_specs=(vmem, vmem),
        scratch_shapes=[
            pltpu.VMEM((2, rows, m), jnp.bfloat16),
            pltpu.VMEM((n_grid, 2, 2, half, w), jnp.bfloat16),
            pltpu.VMEM((2, rows, w), jnp.float32),
            pltpu.VMEM((n_pole, cap, rows), jnp.bfloat16),
            pltpu.VMEM((n_pole // 2, cap, w), jnp.bfloat16),
            pltpu.VMEM((n_pole // 2, cap, w), jnp.bfloat16),
            pltpu.VMEM((n_pole // 2, cap, w), jnp.float32),
            pltpu.VMEM((n_pole // 2 - 1, cap, w), jnp.bfloat16),
            pltpu.VMEM((n_pole // 2 - 1, cap, w), jnp.bfloat16),
            pltpu.VMEM((w, w), jnp.float32),
            pltpu.VMEM((n_grid, sub, w), jnp.bfloat16),
            pltpu.VMEM((n_grid - 1, sub, w), jnp.bfloat16),
            pltpu.VMEM((n_pole, sub, w), jnp.float32),
            dma((2,)),
            dma((4,)),
            dma((n_grid * 6,)),
            dma((n_grid * 2,)),
            dma((2,)),
            dma((n_pole // 2 - 1,)),
            dma((n_pole // 2 - 1,)),
            dma((n_grid - 1,)),
            dma((n_grid - 1,)),
            dma((n_pole - 1,)),
            dma((n_pole - 1,)),
        ],
        compiler_params=pltpu.CompilerParams(
            collective_id=0, has_side_effects=True, vmem_limit_bytes=60 * 1024 * 1024
        ),
        cost_estimate=pl.CostEstimate(
            flops=8 * rows * m * w, bytes_accessed=4 * rows * m, transcendentals=0
        ),
    )(trailing, panel, pole_weights, owner_map.reshape(1, rows), diag_inverse)
    patch_energy = jnp.dot(patch, ham_slab, preferred_element_type=jnp.float32).astype(jnp.bfloat16)
    return (density_diag, patch_energy)


def solution(mesh):
    n_pole, n_grid = mesh.shape["pole"], mesh.shape["grid"]
    placed = (
        P("pole", None, "grid", None),
        P("pole", None, "grid", None),
        P("pole", None, "grid", None),
        P("pole", None),
        P("grid", None),
        P(),
    )

    def body(trailing, panel, *rest):
        rows, w = panel.shape[2:]
        fits = (
            panel.shape[0] == 1
            and n_pole % 2 == 0
            and 4 <= n_pole <= 16
            and n_grid >= 4
            and n_grid % 2 == 0
            and rows % 256 == 0
            and (2 * rows // n_pole) % 16 == 0
            and w % (16 * n_grid) == 0
            and w % 128 == 0
        )
        if fits:
            return per_device(n_pole, n_grid, trailing, panel, *rest)
        return per_device_small(trailing, panel, *rest)

    return jax.shard_map(
        body,
        mesh=mesh,
        in_specs=placed,
        out_specs=(P("grid", None), P(("pole", "grid"), None)),
        check_vma=False,
    )
```

```python
import functools

import jax
import jax.numpy as jnp
from jax import lax
from jax.experimental import pallas as pl
from jax.experimental.pallas import tpu as pltpu
from jax.sharding import PartitionSpec as P

MESH = pl.DeviceIdType.MESH
LAG = 4
CUTS = 4


def complex_product(left_real, left_imag, right_real, right_imag, form):

    def product(first, second):
        return jnp.einsum(form, first, second, preferred_element_type=jnp.float32)

    real = product(left_real, right_real) - product(left_imag, right_imag)
    imag = product(left_real, right_imag) + product(left_imag, right_real)
    return (real, imag)


def per_device_small(trailing, panel, diag_inverse, pole_weights, owner_map, ham_slab):
    rows_here = trailing.shape[2]
    piece = lax.all_gather(panel, "grid", axis=2, tiled=True)
    real, imag = complex_product(
        trailing[:, 0], trailing[:, 1], piece[:, 0], piece[:, 1], "prn,pnw->prw"
    )
    cross_real = (-real).astype(jnp.bfloat16)
    cross_imag = (-imag).astype(jnp.bfloat16)
    weight_real = pole_weights[:, 0][:, None, None]
    weight_imag = pole_weights[:, 1][:, None, None]
    density_rows = jnp.sum(
        weight_real * cross_imag.astype(jnp.float32) + weight_imag * cross_real.astype(jnp.float32),
        axis=0,
    )
    quad_real, quad_imag = complex_product(
        panel[:, 0], panel[:, 1], cross_real, cross_imag, "prw,prv->pwv"
    )
    quad_part = -jnp.sum(weight_real * quad_imag + weight_imag * quad_real, axis=0)
    diag_term = jnp.sum(
        weight_real * diag_inverse[:, 1].astype(jnp.float32)
        + weight_imag * diag_inverse[:, 0].astype(jnp.float32),
        axis=0,
    )
    mine = lax.psum_scatter(quad_part, "grid", scatter_dimension=0, tiled=True) + diag_term
    density_diag = lax.psum(mine, "pole")
    owners = owner_map[:, 0]
    capacity = 2 * rows_here // lax.axis_size("pole")
    same = owners[:, None] == owners[None, :]
    earlier = lax.broadcasted_iota(jnp.int32, (rows_here, rows_here), 1) < lax.broadcasted_iota(
        jnp.int32, (rows_here, rows_here), 0
    )
    rank = jnp.sum((same & earlier).astype(jnp.int32), axis=1)
    slot = owners * capacity + rank
    all_slots = lax.axis_size("pole") * capacity
    placement = (
        slot[:, None] == lax.broadcasted_iota(jnp.int32, (rows_here, all_slots), 1)
    ).astype(jnp.float32)
    total_rows = lax.psum(density_rows, "pole")
    chosen = lax.dynamic_slice_in_dim(placement, lax.axis_index("pole") * capacity, capacity, 1)
    owned_rows = jnp.einsum("rs,rw->sw", chosen, total_rows, precision=lax.Precision.HIGHEST)
    patch = owned_rows.astype(jnp.bfloat16)
    patch_energy = jnp.dot(patch, ham_slab, preferred_element_type=jnp.float32).astype(jnp.bfloat16)
    return (density_diag, patch_energy)


def dot(first, second, over_first=1):
    return lax.dot_general(
        first, second, (((over_first,), (0,)), ((), ())), preferred_element_type=jnp.float32
    )


def kernel(
    n_pole, n_grid, trailing, panel, weights, owners, diag, patch_ref, dd_ref,
    gbuf, lbuf, acc, place, packed, mbuf, sums, pbuf, rbuf, qbuf, abuf, bbuf, obuf,
    gsem, lsem, fwd_send, fwd_recv, m_sem, p_send, p_recv, a_send, a_recv, c_send, c_recv,
):
    ny = 2
    nz = n_grid // ny
    rows = gbuf.shape[1]
    half = rows // CUTS
    cap = rbuf.shape[1]
    sub, w = obuf.shape[1:]
    pole, me = lax.axis_index("pole"), lax.axis_index("grid")
    z, y = me // ny, me % ny

    gcopies = [
        pltpu.make_async_copy(trailing.at[0, c], gbuf.at[c], gsem.at[c]) for c in range(2)
    ]
    lcopies = [
        pltpu.make_async_copy(
            panel.at[0, c, pl.ds(h * half, half)], lbuf.at[me, h, c], lsem.at[2 * h + c]
        )
        for h in range(CUTS)
        for c in range(2)
    ]
    for copy in lcopies + gcopies:
        copy.start()

    barrier = pltpu.get_barrier_semaphore()
    for k in range(1, n_grid):
        pl.semaphore_signal(
            barrier, inc=1, device_id=(pole, lax.rem(me + k, n_grid)), device_id_type=MESH
        )
    for k in range(1, n_pole):
        pl.semaphore_signal(
            barrier, inc=1, device_id=(lax.rem(pole + k, n_pole), me), device_id_type=MESH
        )

    names = lax.broadcasted_iota(jnp.int32, (16, rows), 0) == owners[...]
    ones = names.astype(jnp.float32)
    before = (
        lax.broadcasted_iota(jnp.int32, (rows, rows), 0)
        < lax.broadcasted_iota(jnp.int32, (rows, rows), 1)
    ).astype(jnp.float32)
    counts = dot(ones.astype(jnp.bfloat16), before.astype(jnp.bfloat16))
    rank = jnp.sum(ones * counts, axis=0, keepdims=True).astype(jnp.int32)
    slot = owners[...] * cap + rank
    for q in range(n_pole):
        here = lax.broadcasted_iota(jnp.int32, (cap, rows), 0) + q * cap == slot
        place[q] = here.astype(jnp.float32).astype(jnp.bfloat16)
    acc[...] = jnp.zeros_like(acc)

    for copy in lcopies:
        copy.wait()
    pl.semaphore_wait(barrier, n_grid - 1 + n_pole - 1)

    def sends(kind, d, h, s, src):
        own_line = kind == 0
        first = d == 0
        src_z = src // ny
        turn = (kind == 1) & (h < CUTS // 2)
        turn_up = turn & jnp.where(z + 1 == nz - 1, src_z == 0, first)
        turn_down = turn & jnp.where(z == 1, src_z == nz - 1, first)
        up = (z + 1 < nz) & ((own_line & (first | (s == -1))) | turn_up)
        down = (z >= 1) & ((own_line & (first | (s == 1))) | turn_down)
        spared = jnp.where((z == 0) | (z == nz - 1), nz - 1, 1)
        over = own_line & jnp.logical_not((d == spared) & (h < CUTS // 2))
        targets = (jnp.minimum(z + 1, nz - 1) * ny + y, jnp.maximum(z - 1, 0) * ny + y, z * ny + 1 - y)
        out = []
        for j, (cond, target) in enumerate(zip((up, down, over), targets)):
            out.append((cond, pltpu.make_async_remote_copy(
                src_ref=lbuf.at[src, h],
                dst_ref=lbuf.at[src, h],
                send_sem=fwd_send.at[(src * CUTS + h) * 3 + j],
                recv_sem=fwd_recv.at[src * CUTS + h],
                device_id=(pole, target),
                device_id_type=MESH,
            )))
        return out

    def event(i):
        t, r = i // 4, i % 4
        kind, side = r // 2, r % 2
        tt = jnp.maximum(t - kind * LAG, 0)
        d, h = tt // CUTS, tt % CUTS
        s = 1 - 2 * side
        src_z = z + s * d
        valid = (t >= kind * LAG) & (t - kind * LAG < CUTS * nz) & (src_z >= 0) & (src_z < nz)
        valid = valid & jnp.logical_not((d == 0) & (side == 1))
        src = jnp.clip(src_z, 0, nz - 1) * ny + jnp.where(kind == 0, y, 1 - y)
        return valid, kind, d, h, s, src

    zero = jnp.int32(0)
    for h in range(CUTS):
        for cond, copy in sends(zero, zero, jnp.int32(h), jnp.int32(1), me):
            pl.when(cond)(copy.start)
    for copy in gcopies:
        copy.wait()

    def step(i, carry):
        valid, kind, d, h, s, src = event(i)

        @pl.when(valid)
        def _():
            @pl.when((d > 0) | (kind == 1))
            def _():
                pltpu.make_async_remote_copy(
                    src_ref=lbuf.at[src, h],
                    dst_ref=lbuf.at[src, h],
                    send_sem=fwd_send.at[(src * CUTS + h) * 3],
                    recv_sem=fwd_recv.at[src * CUTS + h],
                    device_id=(pole, z * ny + 1 - y),
                    device_id_type=MESH,
                ).wait_recv()
                for cond, copy in sends(kind, d, h, s, src):
                    pl.when(cond)(copy.start)

            cols = pl.ds(pl.multiple_of(src * rows + h * half, half), half)
            g_r, g_i = gbuf[0, :, cols], gbuf[1, :, cols]
            l_r, l_i = lbuf[src, h, 0], lbuf[src, h, 1]
            acc[0] += dot(g_r, l_r) - dot(g_i, l_i)
            acc[1] += dot(g_r, l_i) + dot(g_i, l_r)

        return carry

    lax.fori_loop(0, 4 * (CUTS * nz + LAG), step, 0)

    w_r, w_i = weights[0, 0], weights[0, 1]
    x_r, x_i = -acc[0], -acc[1]
    dens = (w_r * x_i + w_i * x_r).astype(jnp.bfloat16)
    other = (w_r * x_r - w_i * x_i).astype(jnp.bfloat16)

    core, cap_sets = pole % 2, n_pole // 2
    mate = pole + 1 - 2 * core
    for j in range(cap_sets):
        packed[j] = dot(place[2 * j + 1 - core], dens).astype(jnp.bfloat16)
    mate_copy = pltpu.make_async_remote_copy(
        src_ref=packed, dst_ref=mbuf, send_sem=m_sem.at[0], recv_sem=m_sem.at[1],
        device_id=(mate, me), device_id_type=MESH,
    )
    mate_copy.start()

    quad = jnp.zeros((w, w), jnp.float32)
    for h in range(CUTS):
        part = slice(h * half, (h + 1) * half)
        quad += dot(lbuf[me, h, 0], dens[part], 0) + dot(lbuf[me, h, 1], other[part], 0)
    qbuf[...] = -quad
    for g in range(n_grid):
        abuf[g] = qbuf[g * sub:(g + 1) * sub].astype(jnp.bfloat16)
    a_copies = []
    for k in range(1, n_grid):
        g = lax.rem(me + k, n_grid)
        a_copies.append(pltpu.make_async_remote_copy(
            src_ref=abuf.at[g], dst_ref=bbuf.at[k - 1],
            send_sem=a_send.at[k - 1], recv_sem=a_recv.at[k - 1],
            device_id=(pole, g), device_id_type=MESH,
        ))
        a_copies[-1].start()
    term = w_r * diag[0, 1].astype(jnp.float32) + w_i * diag[0, 0].astype(jnp.float32)
    final = term + qbuf[pl.ds(pl.multiple_of(me * sub, sub), sub)]
    for j in range(cap_sets):
        sums[j] = dot(place[2 * j + core], dens)

    mate_copy.wait_recv()
    p_copies = []
    for k in range(1, cap_sets):
        j = lax.rem(pole // 2 + k, cap_sets)
        pbuf[k - 1] = (sums[j] + mbuf[j].astype(jnp.float32)).astype(jnp.bfloat16)
        p_copies.append(pltpu.make_async_remote_copy(
            src_ref=pbuf.at[k - 1], dst_ref=rbuf.at[k - 1],
            send_sem=p_send.at[k - 1], recv_sem=p_recv.at[k - 1],
            device_id=(2 * j + core, me), device_id_type=MESH,
        ))
        p_copies[-1].start()
    owned = sums[pole // 2] + mbuf[pole // 2].astype(jnp.float32)

    for k in range(1, n_grid):
        a_copies[k - 1].wait_recv()
        final += bbuf[k - 1].astype(jnp.float32)
    obuf[pole] = final
    c_copies = []
    for k in range(1, n_pole):
        c_copies.append(pltpu.make_async_remote_copy(
            src_ref=obuf.at[pole], dst_ref=obuf.at[pole],
            send_sem=c_send.at[k - 1], recv_sem=c_recv.at[k - 1],
            device_id=(lax.rem(pole + k, n_pole), me), device_id_type=MESH,
        ))
        c_copies[-1].start()

    def drain(i, carry):
        valid, kind, d, h, s, src = event(i)
        for cond, copy in sends(kind, d, h, s, src):
            pl.when(valid & cond)(copy.wait_send)
        return carry

    lax.fori_loop(0, 4 * (CUTS * nz + LAG), drain, 0)
    mate_copy.wait_send()
    for copy in p_copies:
        copy.wait()
    for k in range(1, cap_sets):
        owned += rbuf[k - 1].astype(jnp.float32)
    patch_ref[...] = owned.astype(jnp.bfloat16)
    for copy in a_copies:
        copy.wait_send()
    for k in range(1, n_pole):
        c_copies[k - 1].wait()
    result = obuf[0]
    for p in range(1, n_pole):
        result += obuf[p]
    dd_ref[...] = result


def per_device(n_pole, n_grid, trailing, panel, diag_inverse, pole_weights, owner_map, ham_slab):
    rows, m = trailing.shape[2:]
    w = panel.shape[3]
    half = rows // CUTS
    cap = 2 * rows // n_pole
    sub = w // n_grid
    vmem = pl.BlockSpec(memory_space=pltpu.VMEM)
    dma = pltpu.SemaphoreType.DMA
    patch, density_diag = pl.pallas_call(
        functools.partial(kernel, n_pole, n_grid),
        out_shape=(
            jax.ShapeDtypeStruct((cap, w), jnp.bfloat16),
            jax.ShapeDtypeStruct((w // n_grid, w), jnp.float32),
        ),
        in_specs=[
            pl.BlockSpec(memory_space=pl.ANY),
            pl.BlockSpec(memory_space=pl.ANY),
            pl.BlockSpec(memory_space=pltpu.SMEM),
            vmem,
            vmem,
        ],
        out_specs=(vmem, vmem),
        scratch_shapes=[
            pltpu.VMEM((2, rows, m), jnp.bfloat16),
            pltpu.VMEM((n_grid, CUTS, 2, half, w), jnp.bfloat16),
            pltpu.VMEM((2, rows, w), jnp.float32),
            pltpu.VMEM((n_pole, cap, rows), jnp.bfloat16),
            pltpu.VMEM((n_pole // 2, cap, w), jnp.bfloat16),
            pltpu.VMEM((n_pole // 2, cap, w), jnp.bfloat16),
            pltpu.VMEM((n_pole // 2, cap, w), jnp.float32),
            pltpu.VMEM((n_pole // 2 - 1, cap, w), jnp.bfloat16),
            pltpu.VMEM((n_pole // 2 - 1, cap, w), jnp.bfloat16),
            pltpu.VMEM((w, w), jnp.float32),
            pltpu.VMEM((n_grid, sub, w), jnp.bfloat16),
            pltpu.VMEM((n_grid - 1, sub, w), jnp.bfloat16),
            pltpu.VMEM((n_pole, sub, w), jnp.float32),
            dma((2,)),
            dma((2 * CUTS,)),
            dma((n_grid * CUTS * 3,)),
            dma((n_grid * CUTS,)),
            dma((2,)),
            dma((n_pole // 2 - 1,)),
            dma((n_pole // 2 - 1,)),
            dma((n_grid - 1,)),
            dma((n_grid - 1,)),
            dma((n_pole - 1,)),
            dma((n_pole - 1,)),
        ],
        compiler_params=pltpu.CompilerParams(
            collective_id=0, has_side_effects=True, vmem_limit_bytes=60 * 1024 * 1024
        ),
        cost_estimate=pl.CostEstimate(
            flops=8 * rows * m * w, bytes_accessed=4 * rows * m, transcendentals=0
        ),
    )(trailing, panel, pole_weights, owner_map.reshape(1, rows), diag_inverse)
    patch_energy = jnp.dot(patch, ham_slab, preferred_element_type=jnp.float32).astype(jnp.bfloat16)
    return (density_diag, patch_energy)


def solution(mesh):
    n_pole, n_grid = mesh.shape["pole"], mesh.shape["grid"]
    placed = (
        P("pole", None, "grid", None),
        P("pole", None, "grid", None),
        P("pole", None, "grid", None),
        P("pole", None),
        P("grid", None),
        P(),
    )

    def body(trailing, panel, *rest):
        rows, w = panel.shape[2:]
        fits = (
            panel.shape[0] == 1
            and n_pole % 2 == 0
            and 4 <= n_pole <= 16
            and n_grid >= 4
            and n_grid % 2 == 0
            and rows % (128 * CUTS) == 0
            and (2 * rows // n_pole) % 16 == 0
            and w % (16 * n_grid) == 0
            and w % 128 == 0
        )
        if fits:
            return per_device(n_pole, n_grid, trailing, panel, *rest)
        return per_device_small(trailing, panel, *rest)

    return jax.shard_map(
        body,
        mesh=mesh,
        in_specs=placed,
        out_specs=(P("grid", None), P(("pole", "grid"), None)),
        check_vma=False,
    )
```
